32 devices in a mesh: parts: 2 (over y), col: 4 (over z), row: 4 (over x, core).
Axes of the slice: x: 2, y: 2, z: 4, core: 2. Of those that a mesh axis runs over, the one named last changes fastest.
Arguments:
- grad_table: bfloat16 [16384, 32768], P(('parts', 'row'), 'col'), parts along dimension 0, may hold values from -60 to 60
- prev_embed: bfloat16 [8192, 512], P('row', 'col'), may hold values from -6 to 6
- next_embed: bfloat16 [32768, 512], P('col', 'row'), may hold values from -6 to 6
- log_norm: float32 [16384], P(('parts', 'row')), parts along dimension 0, may hold values from 9 to 11
Outputs:
- prev_grad: float32 [16384, 512], P(('parts', 'row'), 'col'), parts along dimension 0
- next_grad: float32 [65536, 512], P(('parts', 'col'), 'row'), parts along dimension 0
The draws below stay inside these ranges and needn't reach their ends.
There are 2 independent parts, one for each index of `parts`. The reference program is written for one: setup_inputs(seed, part) draws one part's arguments, and reference() takes and returns one part's arrays. A program takes and returns all parts, laid end to end along the dimension named above; an argument that names none is the same for every part. Nothing has to cross between parts.
All inputs are finite; a program needn't handle non-finite values.
Results may differ from the reference program's by a relative error of at most 0.0025.
Values may be sent and summed in bfloat16 or wider, within the bound.
A program may use at most 256 MiB of HBM per device.

```python
import math
import jax
import jax.numpy as jnp
from jax import lax

E = 512
NEXT = 32768
ROWS = 8192


def steps_of(own_key, extent, cuts, least, top_value):
    factor_of, own = 1.0, jax.random.fold_in(own_key, 6)
    for dim, blocks in cuts:
        steps = jnp.exp(jax.random.uniform(jax.random.fold_in(own, dim), (blocks,), jnp.float32, least / len(cuts), top_value / len(cuts)))
        factor_of = factor_of * jnp.repeat(steps, extent[dim] // blocks).reshape([-1 if axis == dim else 1 for axis in range(len(extent))])
    return factor_of


def gaussian(rng, extent, deviation, most, shards=(), kind=jnp.bfloat16):
    array = jax.random.normal(rng, extent, jnp.float32) * deviation
    if len(shards) > 0:
        array = steps_of(rng, extent, shards, -0.22, 0.18) * array
    return jnp.clip(array, min=-most, max=most).astype(kind)


def setup_inputs(seed: int = 0, part: int = 0) -> dict:
    key_of = jax.random.split(jax.random.key(seed), 5)
    part_keys = jax.random.split(jax.random.fold_in(key_of[4], part), 5)
    return {
        "grad_table": gaussian(part_keys[0], (ROWS, NEXT), 10.0, 60.0, ((0, 4), (1, 4))),
        "prev_embed": gaussian(key_of[1], (ROWS, E), 1.0, 6.0, ((0, 4), (1, 4))),
        "next_embed": gaussian(key_of[2], (NEXT, E), 1.0, 6.0, ((0, 4), (1, 4))),
        "log_norm": jnp.clip(9.0 + 2.0 * jax.random.uniform(part_keys[3], (ROWS,), jnp.float32) ** steps_of(part_keys[3], (ROWS,), ((0, 4),), -0.2, 0.2), 9.0, 11.0),
    }


def reference(grad_table, prev_embed, next_embed, log_norm):
    scale = 2.0 / math.sqrt(E)
    block = min(512, ROWS)
    count = ROWS // block

    def step(total, index):
        start = (index * block).astype(jnp.int32)
        upstream = lax.dynamic_slice_in_dim(grad_table, start, block, 0)
        left = lax.dynamic_slice_in_dim(prev_embed, start, block, 0)
        norms = lax.dynamic_slice_in_dim(log_norm, start, block, 0)
        logits = scale * jnp.dot(left, next_embed.T, preferred_element_type=jnp.float32)
        probs = jnp.exp(logits - norms[:, None])
        widened = upstream.astype(jnp.float32)
        row_dot = lax.optimization_barrier(jnp.sum(widened * probs, axis=1, keepdims=True))
        dlogits = (scale * probs * (widened - row_dot)).astype(jnp.bfloat16)
        prev_part = jnp.dot(dlogits, next_embed, preferred_element_type=jnp.float32)
        total = total + jnp.dot(dlogits.T, left, preferred_element_type=jnp.float32)
        return (total, prev_part)
    initial = jnp.zeros((NEXT, E), jnp.float32)
    next_grad, prev_parts = lax.scan(step, initial, jnp.arange(count, dtype=jnp.int32))
    return (prev_parts.reshape(ROWS, E), next_grad)
```

```python
import functools
import math

import jax
import jax.numpy as jnp
from jax import lax
from jax.experimental import pallas as pl
from jax.experimental.pallas import tpu as pltpu
from jax.sharding import PartitionSpec as P

LOG2E = math.log2(math.e)
TILE = 512
ROW_BLOCK = 512
CHUNKS = 4
NT = (((1,), (1,)), ((), ()))


def dots_kernel(coef, grad_ref, prev_ref, next_ref, bias_ref, total_ref, out_ref):
    @pl.when(pl.program_id(0) == 0)
    def _():
        out_ref[...] = total_ref[...]

    rows, width = grad_ref.shape
    block = min(ROW_BLOCK, rows)
    for top in range(0, rows, block):
        here = pl.ds(top, block)
        logits = lax.dot_general(
            prev_ref[here, :], next_ref[...], NT, preferred_element_type=jnp.float32
        )
        terms = grad_ref[here, :].astype(jnp.float32) * jnp.exp2(logits * coef - bias_ref[here, :])
        part = terms[:, :128]
        for left in range(128, width, 128):
            part = part + terms[:, left : left + 128]
        out_ref[here, :] += part


def grads_kernel(
    coef, pieces, grad_ref, prev_ref, prev_t_ref, next_ref, bias_ref, dot_ref, total_ref,
    out_ref, *rest
):
    piece_refs, held = rest[:-1], rest[-1]

    @pl.when(pl.program_id(0) == 0)
    def _():
        out_ref[...] = total_ref[...]

    rows = grad_ref.shape[0]
    block = min(ROW_BLOCK, rows)
    for top in range(0, rows, block):
        here = pl.ds(top, block)
        logits = lax.dot_general(
            prev_ref[here, :], next_ref[...], NT, preferred_element_type=jnp.float32
        )
        scaled = jnp.exp2(logits * coef - bias_ref[here, :])
        shifted = grad_ref[here, :].astype(jnp.float32) - dot_ref[here, :]
        dlogits = (scaled * shifted).astype(jnp.bfloat16)
        held[here, :] = dlogits
        out_ref[here, :] += jnp.dot(dlogits, next_ref[...], preferred_element_type=jnp.float32)
    flipped = jnp.dot(prev_t_ref[...], held[...], preferred_element_type=jnp.float32)
    for (start, size, kind), ref in zip(pieces, piece_refs):
        ref[...] = flipped[start : start + size, :].T.astype(kind)


def row_dots(grad, prev, nxt, bias, total, first, coef):
    rows, features = prev.shape
    columns = nxt.shape[0]
    tile = min(TILE, columns)
    offset = first // tile
    whole = lambda shape: pl.BlockSpec(shape, lambda j: (0, 0))
    return pl.pallas_call(
        functools.partial(dots_kernel, coef),
        grid=(columns // tile,),
        out_shape=jax.ShapeDtypeStruct(total.shape, jnp.float32),
        in_specs=[
            pl.BlockSpec((rows, tile), lambda j: (0, j + offset)),
            whole(prev.shape),
            pl.BlockSpec((tile, features), lambda j: (j, 0)),
            whole(bias.shape),
            whole(total.shape),
        ],
        out_specs=whole(total.shape),
        compiler_params=pltpu.CompilerParams(vmem_limit_bytes=48 << 20),
        cost_estimate=pl.CostEstimate(
            flops=2 * rows * columns * features,
            bytes_accessed=2 * rows * columns,
            transcendentals=rows * columns,
        ),
    )(grad, prev, nxt, bias, total)


def grad_terms(grad, prev, prev_t, nxt, bias, dots, total, first, coef, pieces):
    rows, features = prev.shape
    columns = nxt.shape[0]
    tile = min(TILE, columns)
    offset = first // tile
    whole = lambda shape: pl.BlockSpec(shape, lambda j: (0, 0))
    return pl.pallas_call(
        functools.partial(grads_kernel, coef, pieces),
        grid=(columns // tile,),
        out_shape=[jax.ShapeDtypeStruct(total.shape, jnp.float32)]
        + [jax.ShapeDtypeStruct((columns, size), kind) for _, size, kind in pieces],
        in_specs=[
            pl.BlockSpec((rows, tile), lambda j: (0, j + offset)),
            whole(prev.shape),
            whole(prev_t.shape),
            pl.BlockSpec((tile, features), lambda j: (j, 0)),
            whole(bias.shape),
            whole(dots.shape),
            whole(total.shape),
        ],
        out_specs=[whole(total.shape)]
        + [pl.BlockSpec((tile, size), lambda j: (j, 0)) for _, size, _ in pieces],
        scratch_shapes=[pltpu.VMEM((rows, tile), jnp.bfloat16)],
        compiler_params=pltpu.CompilerParams(vmem_limit_bytes=56 << 20),
        cost_estimate=pl.CostEstimate(
            flops=6 * rows * columns * features,
            bytes_accessed=2 * rows * columns,
            transcendentals=rows * columns,
        ),
    )(grad, prev, prev_t, nxt, bias, dots, total)


def body(cols, grid_rows, grad_table, prev_embed, next_embed, log_norm):
    rows, columns = grad_table.shape
    features = prev_embed.shape[1] * cols
    scale = 2.0 / math.sqrt(features)
    coef = scale * LOG2E
    share = next_embed.shape[1]
    paired = cols == 4 and grid_rows == 4 and share % 128 == 0
    step = columns // CHUNKS if columns % (CHUNKS * TILE) == 0 else columns
    starts = list(range(0, columns, step))
    r, c = lax.axis_index("row"), lax.axis_index("col")

    def swap(x, bit):
        return lax.ppermute(x, "row", [(i, i ^ bit) for i in range(grid_rows)])

    def shift(x, by):
        return lax.ppermute(x, "col", [(i, (i + by) % cols) for i in range(cols)])

    if paired:
        order = (0, 2, 1, 3)
        arrived = jnp.stack([prev_embed] + [shift(prev_embed, cols - a) for a in range(1, cols)])
        prev = jnp.concatenate(
            [
                lax.dynamic_index_in_dim(arrived, ((r ^ o) - c + cols) % cols, 0, keepdims=False)
                for o in order
            ],
            axis=1,
        )
        nexts = []
        for first in starts:
            mine = next_embed[first : first + step]
            across = swap(mine, 2)
            both = jnp.concatenate([mine, across], axis=1)
            nexts.append(jnp.concatenate([both, swap(both, 1)], axis=1))
        pieces = (
            (0, share, jnp.float32),
            (share, share, jnp.float32),
            (2 * share, 2 * share, jnp.bfloat16),
        )
    else:
        prev = lax.all_gather(prev_embed, "col", axis=1, tiled=True)
        gathered = lax.all_gather(next_embed, "row", axis=1, tiled=True)
        nexts = [gathered[first : first + step] for first in starts]
        pieces = ((0, features, jnp.float32),)

    bias = log_norm[:, None] * LOG2E
    total = jnp.zeros((rows, 128), jnp.float32)
    for first, nxt in zip(starts, nexts):
        total = row_dots(grad_table, prev, nxt, bias, total, first, coef)
    dots = lax.psum(jnp.sum(total, axis=1), "col")[:, None]

    prev_t = prev.T
    bias = bias - math.log2(scale)
    total = jnp.zeros((rows, features), jnp.float32)
    ends = []
    for first, nxt in zip(starts, nexts):
        total, *sums = grad_terms(
            grad_table, prev, prev_t, nxt, bias, dots, total, first, coef, pieces
        )
        if paired:
            own, far, give = sums
            got = swap(give, 1).astype(jnp.float32)
            far = swap((far + got[:, share:]).astype(jnp.bfloat16), 2)
            ends.append(own + got[:, :share] + far.astype(jnp.float32))
        else:
            ends.append(lax.psum_scatter(sums[0], "row", scatter_dimension=1, tiled=True))
    next_grad = jnp.concatenate(ends, axis=0)

    if paired:
        def block(col):
            code = jnp.bitwise_xor(col, r)
            place = jnp.where(code == 1, 2, jnp.where(code == 2, 1, code))
            return lax.dynamic_slice_in_dim(total, place * share, share, 1)

        prev_grad = block(c)
        for a in range(1, cols):
            away = block((c + a) % cols).astype(jnp.bfloat16)
            prev_grad = prev_grad + shift(away, a).astype(jnp.float32)
    else:
        prev_grad = lax.psum_scatter(total, "col", scatter_dimension=1, tiled=True)
    return (prev_grad, next_grad)


def solution(mesh):
    placed = (P(("parts", "row"), "col"), P("row", "col"), P("col", "row"), P(("parts", "row")))
    return jax.shard_map(
        functools.partial(body, mesh.shape["col"], mesh.shape["row"]),
        mesh=mesh,
        in_specs=placed,
        out_specs=(P(("parts", "row"), "col"), P(("parts", "col"), "row")),
        check_vma=False,
    )
```

```python
import functools
import math

import jax
import jax.numpy as jnp
from jax import lax
from jax.experimental import pallas as pl
from jax.experimental.pallas import tpu as pltpu
from jax.sharding import PartitionSpec as P

LOG2E = math.log2(math.e)
TILE = 512
ROW_BLOCK = 512
CHUNKS = 4
NT = (((1,), (1,)), ((), ()))


def arrange_kernel(places_ref, arrived_ref, prev_ref, prev_t_ref):
    block = arrived_ref[0, 0]
    prev_ref[...] = block
    prev_t_ref[...] = block.T


def arrange(arrived, places):
    blocks, halves, height, share = arrived.shape
    rows, features = halves * height, blocks * share
    return pl.pallas_call(
        arrange_kernel,
        grid_spec=pltpu.PrefetchScalarGridSpec(
            num_scalar_prefetch=1,
            grid=(blocks, halves),
            in_specs=[
                pl.BlockSpec(
                    (1, 1, height, share),
                    lambda i, h, places: (places[i], places[blocks + h], 0, 0),
                )
            ],
            out_specs=[
                pl.BlockSpec((height, share), lambda i, h, places: (h, i)),
                pl.BlockSpec((share, height), lambda i, h, places: (i, h)),
            ],
        ),
        out_shape=[
            jax.ShapeDtypeStruct((rows, features), arrived.dtype),
            jax.ShapeDtypeStruct((features, rows), arrived.dtype),
        ],
        cost_estimate=pl.CostEstimate(
            flops=0, bytes_accessed=6 * rows * features, transcendentals=0
        ),
    )(places, arrived)


def join(next_refs, held):
    left = 0
    for ref in next_refs:
        held[:, left : left + ref.shape[1]] = ref[...]
        left += ref.shape[1]


def dots_kernel(coef, count, grad_ref, prev_ref, bias_ref, total_ref, *rest):
    next_refs, (out_ref, next_held) = rest[:count], rest[count:]

    @pl.when(pl.program_id(0) == 0)
    def _():
        out_ref[...] = total_ref[...]

    join(next_refs, next_held)
    rows, width = grad_ref.shape
    block = min(ROW_BLOCK, rows)
    for top in range(0, rows, block):
        here = pl.ds(top, block)
        logits = lax.dot_general(
            prev_ref[here, :], next_held[...], NT, preferred_element_type=jnp.float32
        )
        terms = grad_ref[here, :].astype(jnp.float32) * jnp.exp2(logits * coef - bias_ref[here, :])
        part = terms[:, :128]
        for left in range(128, width, 128):
            part = part + terms[:, left : left + 128]
        out_ref[here, :] += part


def grads_kernel(
    coef, pieces, count, grad_ref, prev_ref, prev_t_ref, bias_ref, dot_ref, total_ref, *rest
):
    next_refs = rest[:count]
    out_ref, *piece_refs = rest[count:-2]
    next_held, held = rest[-2:]

    @pl.when(pl.program_id(0) == 0)
    def _():
        out_ref[...] = total_ref[...]

    join(next_refs, next_held)
    rows = grad_ref.shape[0]
    block = min(ROW_BLOCK, rows)
    for top in range(0, rows, block):
        here = pl.ds(top, block)
        logits = lax.dot_general(
            prev_ref[here, :], next_held[...], NT, preferred_element_type=jnp.float32
        )
        scaled = jnp.exp2(logits * coef - bias_ref[here, :])
        shifted = grad_ref[here, :].astype(jnp.float32) - dot_ref[here, :]
        dlogits = (scaled * shifted).astype(jnp.bfloat16)
        held[here, :] = dlogits
        out_ref[here, :] += jnp.dot(dlogits, next_held[...], preferred_element_type=jnp.float32)
    flipped = jnp.dot(prev_t_ref[...], held[...], preferred_element_type=jnp.float32)
    for (start, size, kind), ref in zip(pieces, piece_refs):
        ref[...] = flipped[start : start + size, :].T.astype(kind)


def whole(shape):
    return pl.BlockSpec(shape, lambda j: (0, 0))


def tiles_of(tile, nexts):
    return [
        pl.BlockSpec((tile, x.shape[1]), functools.partial(lambda skip, j: (j + skip, 0), at // tile))
        for x, at in nexts
    ]


def row_dots(grad, prev, nexts, bias, total, first, step, coef):
    rows, features = prev.shape
    tile = min(TILE, step)
    offset = first // tile
    return pl.pallas_call(
        functools.partial(dots_kernel, coef, len(nexts)),
        grid=(step // tile,),
        out_shape=jax.ShapeDtypeStruct(total.shape, jnp.float32),
        in_specs=[
            pl.BlockSpec((rows, tile), lambda j: (0, j + offset)),
            whole(prev.shape),
            whole(bias.shape),
            whole(total.shape),
        ]
        + tiles_of(tile, nexts),
        out_specs=whole(total.shape),
        scratch_shapes=[pltpu.VMEM((tile, features), jnp.bfloat16)],
        compiler_params=pltpu.CompilerParams(vmem_limit_bytes=48 << 20),
        cost_estimate=pl.CostEstimate(
            flops=2 * rows * step * features,
            bytes_accessed=2 * rows * step,
            transcendentals=rows * step,
        ),
    )(grad, prev, bias, total, *[x for x, _ in nexts])


def grad_terms(grad, prev, prev_t, nexts, bias, dots, total, first, step, coef, pieces):
    rows, features = prev.shape
    tile = min(TILE, step)
    offset = first // tile
    return pl.pallas_call(
        functools.partial(grads_kernel, coef, pieces, len(nexts)),
        grid=(step // tile,),
        out_shape=[jax.ShapeDtypeStruct(total.shape, jnp.float32)]
        + [jax.ShapeDtypeStruct((step, size), kind) for _, size, kind in pieces],
        in_specs=[
            pl.BlockSpec((rows, tile), lambda j: (0, j + offset)),
            whole(prev.shape),
            whole(prev_t.shape),
            whole(bias.shape),
            whole(dots.shape),
            whole(total.shape),
        ]
        + tiles_of(tile, nexts),
        out_specs=[whole(total.shape)]
        + [pl.BlockSpec((tile, size), lambda j: (j, 0)) for _, size, _ in pieces],
        scratch_shapes=[
            pltpu.VMEM((tile, features), jnp.bfloat16),
            pltpu.VMEM((rows, tile), jnp.bfloat16),
        ],
        compiler_params=pltpu.CompilerParams(vmem_limit_bytes=56 << 20),
        cost_estimate=pl.CostEstimate(
            flops=6 * rows * step * features,
            bytes_accessed=2 * rows * step,
            transcendentals=rows * step,
        ),
    )(grad, prev, prev_t, bias, dots, total, *[x for x, _ in nexts])


def body(parts, cols, grid_rows, grad_table, prev_embed, next_embed, log_norm):
    rows, columns = grad_table.shape
    features = prev_embed.shape[1] * cols
    scale = 2.0 / math.sqrt(features)
    coef = scale * LOG2E
    share = next_embed.shape[1]
    paired = parts == 2 and cols == 4 and grid_rows == 4 and share % 128 == 0
    step = columns // CHUNKS if columns % (CHUNKS * TILE) == 0 else columns
    starts = list(range(0, columns, step))
    r, c, p = lax.axis_index("row"), lax.axis_index("col"), lax.axis_index("parts")

    def swap(x, bit):
        return lax.ppermute(x, "row", [(i, i ^ bit) for i in range(grid_rows)])

    def shift(x, by):
        return lax.ppermute(x, "col", [(i, (i + by) % cols) for i in range(cols)])

    def trade(x):
        return lax.ppermute(x, "parts", [(0, 1), (1, 0)])

    if paired:
        half = rows // 2
        mine = lax.dynamic_slice_in_dim(prev_embed, p * half, half, 0)
        other = lax.dynamic_slice_in_dim(prev_embed, (1 - p) * half, half, 0)
        arrived = [mine, other]
        for a in range(1, cols):
            near = shift(mine, cols - a)
            arrived += [near, trade(near)]
        beside = swap(next_embed, 1)
        across = [swap(next_embed[first : first + step], 2) for first in starts]
        corner = [swap(x, 1) for x in across]
        nexts = [
            [(next_embed, first), (x, 0), (beside, first), (y, 0)]
            for first, x, y in zip(starts, across, corner)
        ]
        places = [((r ^ o) - c + cols) % cols for o in (0, 2, 1, 3)] + [p, 1 - p]
        arrived = jnp.stack(arrived).reshape(cols, 2, half, share)
        prev, prev_t = arrange(arrived, jnp.stack(places).astype(jnp.int32))
        pieces = (
            (0, share, jnp.float32),
            (share, share, jnp.float32),
            (2 * share, 2 * share, jnp.bfloat16),
        )
    else:
        prev = lax.all_gather(prev_embed, "col", axis=1, tiled=True)
        prev_t = prev.T
        gathered = lax.all_gather(next_embed, "row", axis=1, tiled=True)
        nexts = [[(gathered, first)] for first in starts]
        pieces = ((0, features, jnp.float32),)

    bias = log_norm[:, None] * LOG2E
    total = jnp.zeros((rows, 128), jnp.float32)
    for first, nxt in zip(starts, nexts):
        total = row_dots(grad_table, prev, nxt, bias, total, first, step, coef)
    dots = jnp.sum(total, axis=1)
    if paired:
        mine = dots.reshape(rows // 128, 128)
        dots = (mine + sum(shift(mine, a) for a in range(1, cols))).reshape(rows)
    else:
        dots = lax.psum(dots, "col")
    dots = dots[:, None]

    bias = bias - math.log2(scale)
    total = jnp.zeros((rows, features), jnp.float32)
    ends, sent = [], []
    for k, (first, nxt) in enumerate(zip(starts, nexts)):
        if paired and k >= 2:
            total, sent[k - 2] = lax.optimization_barrier((total, sent[k - 2]))
        if paired and k >= 3:
            total, ends[k - 3] = lax.optimization_barrier((total, ends[k - 3]))
        total, *sums = grad_terms(
            grad_table, prev, prev_t, nxt, bias, dots, total, first, step, coef, pieces
        )
        if paired:
            own, far, give = sums
            got = swap(give, 1)
            sent.append((far + got[:, share:].astype(jnp.float32)).astype(jnp.bfloat16))
            ends.append(own + got[:, :share].astype(jnp.float32))
            if k >= 1:
                ends[k - 1] = ends[k - 1] + swap(sent[k - 1], 2).astype(jnp.float32)
        else:
            ends.append(lax.psum_scatter(sums[0], "row", scatter_dimension=1, tiled=True))
    if paired:
        ends[-1] = ends[-1] + swap(sent[-1], 2).astype(jnp.float32)
    next_grad = jnp.concatenate(ends, axis=0)

    if paired:
        def block(col):
            code = jnp.bitwise_xor(col, r)
            place = jnp.where(code == 1, 2, jnp.where(code == 2, 1, code))
            return lax.dynamic_slice_in_dim(total, place * share, share, 1)

        prev_grad = block(c)
        for a in range(1, cols):
            away = block((c + a) % cols).astype(jnp.bfloat16)
            prev_grad = prev_grad + shift(away, a).astype(jnp.float32)
    else:
        prev_grad = lax.psum_scatter(total, "col", scatter_dimension=1, tiled=True)
    return (prev_grad, next_grad)


def solution(mesh):
    placed = (P(("parts", "row"), "col"), P("row", "col"), P("col", "row"), P(("parts", "row")))
    return jax.shard_map(
        functools.partial(body, *(mesh.shape[axis] for axis in ("parts", "col", "row"))),
        mesh=mesh,
        in_specs=placed,
        out_specs=(P(("parts", "row"), "col"), P(("parts", "col"), "row")),
        check_vma=False,
    )
```

```python
import functools
import math

import jax
import jax.numpy as jnp
from jax import lax
from jax.experimental import pallas as pl
from jax.experimental.pallas import tpu as pltpu
from jax.sharding import PartitionSpec as P

LOG2E = math.log2(math.e)
TILE = 512
ROW_BLOCK = 512
CHUNKS = 4
NT = (((1,), (1,)), ((), ()))


def arrange_kernel(places_ref, arrived_ref, prev_ref, prev_t_ref):
    block = arrived_ref[0, 0]
    prev_ref[...] = block
    prev_t_ref[...] = block.T


def arrange(arrived, places):
    blocks, halves, height, share = arrived.shape
    rows, features = halves * height, blocks * share
    return pl.pallas_call(
        arrange_kernel,
        grid_spec=pltpu.PrefetchScalarGridSpec(
            num_scalar_prefetch=1,
            grid=(blocks, halves),
            in_specs=[
                pl.BlockSpec(
                    (1, 1, height, share),
                    lambda i, h, places: (places[i], places[blocks + h], 0, 0),
                )
            ],
            out_specs=[
                pl.BlockSpec((height, share), lambda i, h, places: (h, i)),
                pl.BlockSpec((share, height), lambda i, h, places: (i, h)),
            ],
        ),
        out_shape=[
            jax.ShapeDtypeStruct((rows, features), arrived.dtype),
            jax.ShapeDtypeStruct((features, rows), arrived.dtype),
        ],
        cost_estimate=pl.CostEstimate(
            flops=0, bytes_accessed=6 * rows * features, transcendentals=0
        ),
    )(places, arrived)


def join(next_refs, held):
    left = 0
    for ref in next_refs:
        held[:, left : left + ref.shape[1]] = ref[...]
        left += ref.shape[1]


def dots_kernel(coef, count, grad_ref, prev_ref, bias_ref, total_ref, *rest):
    next_refs, (out_ref, next_held) = rest[:count], rest[count:]

    @pl.when(pl.program_id(0) == 0)
    def _():
        out_ref[...] = total_ref[...]

    join(next_refs, next_held)
    rows, width = grad_ref.shape
    block = min(ROW_BLOCK, rows)
    for top in range(0, rows, block):
        here = pl.ds(top, block)
        logits = lax.dot_general(
            prev_ref[here, :], next_held[...], NT, preferred_element_type=jnp.float32
        )
        terms = grad_ref[here, :].astype(jnp.float32) * jnp.exp2(logits * coef - bias_ref[here, :])
        part = terms[:, :128]
        for left in range(128, width, 128):
            part = part + terms[:, left : left + 128]
        out_ref[here, :] += part


def grads_kernel(
    coef, pieces, count, carried, grad_ref, prev_ref, prev_t_ref, bias_ref, dot_ref, total_ref, *rest
):
    next_refs = rest[:count]
    out_ref, *piece_refs = rest[count + carried : -2]
    next_held, held = rest[-2:]

    @pl.when(pl.program_id(0) == 0)
    def _():
        out_ref[...] = total_ref[...]

    join(next_refs, next_held)
    rows = grad_ref.shape[0]
    block = min(ROW_BLOCK, rows)
    for top in range(0, rows, block):
        here = pl.ds(top, block)
        logits = lax.dot_general(
            prev_ref[here, :], next_held[...], NT, preferred_element_type=jnp.float32
        )
        scaled = jnp.exp2(logits * coef - bias_ref[here, :])
        shifted = grad_ref[here, :].astype(jnp.float32) - dot_ref[here, :]
        dlogits = (scaled * shifted).astype(jnp.bfloat16)
        held[here, :] = dlogits
        out_ref[here, :] += jnp.dot(dlogits, next_held[...], preferred_element_type=jnp.float32)
    flipped = jnp.dot(prev_t_ref[...], held[...], preferred_element_type=jnp.float32)
    for (start, size, kind), ref in zip(pieces, piece_refs):
        value = flipped[start : start + size, :].T
        if carried:
            value = value + rest[count][:, start : start + size]
        ref[...] = value.astype(kind)


def whole(shape):
    return pl.BlockSpec(shape, lambda j: (0, 0))


def tiles_of(tile, nexts):
    return [
        pl.BlockSpec((tile, x.shape[1]), functools.partial(lambda skip, j: (j + skip, 0), at // tile))
        for x, at in nexts
    ]


def row_dots(grad, prev, nexts, bias, total, first, step, coef):
    rows, features = prev.shape
    tile = min(TILE, step)
    offset = first // tile
    return pl.pallas_call(
        functools.partial(dots_kernel, coef, len(nexts)),
        grid=(step // tile,),
        out_shape=jax.ShapeDtypeStruct(total.shape, jnp.float32),
        in_specs=[
            pl.BlockSpec((rows, tile), lambda j: (0, j + offset)),
            whole(prev.shape),
            whole(bias.shape),
            whole(total.shape),
        ]
        + tiles_of(tile, nexts),
        out_specs=whole(total.shape),
        scratch_shapes=[pltpu.VMEM((tile, features), jnp.bfloat16)],
        compiler_params=pltpu.CompilerParams(vmem_limit_bytes=48 << 20),
        cost_estimate=pl.CostEstimate(
            flops=2 * rows * step * features,
            bytes_accessed=2 * rows * step,
            transcendentals=rows * step,
        ),
    )(grad, prev, bias, total, *[x for x, _ in nexts])


def grad_terms(
    grad, prev, prev_t, nexts, bias, dots, total, first, step, coef, pieces,
    carry=(), split=1, part=0,
):
    features = prev.shape[1]
    rows = prev.shape[0] // split
    tile = min(TILE, step)
    offset = first // tile
    tall = lambda width: pl.BlockSpec((rows, width), lambda j: (part, 0))
    shape = (rows, features)
    return pl.pallas_call(
        functools.partial(grads_kernel, coef, pieces, len(nexts), len(carry)),
        grid=(step // tile,),
        out_shape=[jax.ShapeDtypeStruct(shape, jnp.float32)]
        + [jax.ShapeDtypeStruct((step, size), kind) for _, size, kind in pieces],
        in_specs=[
            pl.BlockSpec((rows, tile), lambda j: (part, j + offset)),
            tall(features),
            pl.BlockSpec((features, rows), lambda j: (0, part)),
            tall(1),
            tall(1),
            tall(features),
        ]
        + tiles_of(tile, nexts)
        + [pl.BlockSpec((tile, features), lambda j: (j, 0)) for _ in carry],
        out_specs=[whole(shape)]
        + [pl.BlockSpec((tile, size), lambda j: (j, 0)) for _, size, _ in pieces],
        scratch_shapes=[
            pltpu.VMEM((tile, features), jnp.bfloat16),
            pltpu.VMEM((rows, tile), jnp.bfloat16),
        ],
        compiler_params=pltpu.CompilerParams(vmem_limit_bytes=56 << 20),
        cost_estimate=pl.CostEstimate(
            flops=6 * rows * step * features,
            bytes_accessed=2 * rows * step,
            transcendentals=rows * step,
        ),
    )(grad, prev, prev_t, bias, dots, total, *[x for x, _ in nexts], *carry)


def body(parts, cols, grid_rows, grad_table, prev_embed, next_embed, log_norm):
    rows, columns = grad_table.shape
    features = prev_embed.shape[1] * cols
    scale = 2.0 / math.sqrt(features)
    coef = scale * LOG2E
    share = next_embed.shape[1]
    paired = parts == 2 and cols == 4 and grid_rows == 4 and share % 128 == 0
    step = columns // CHUNKS if columns % (CHUNKS * TILE) == 0 else columns
    starts = list(range(0, columns, step))
    r, c, p = lax.axis_index("row"), lax.axis_index("col"), lax.axis_index("parts")

    def swap(x, bit):
        return lax.ppermute(x, "row", [(i, i ^ bit) for i in range(grid_rows)])

    def shift(x, by):
        return lax.ppermute(x, "col", [(i, (i + by) % cols) for i in range(cols)])

    def trade(x):
        return lax.ppermute(x, "parts", [(0, 1), (1, 0)])

    if paired:
        half = rows // 2
        mine = lax.dynamic_slice_in_dim(prev_embed, p * half, half, 0)
        other = lax.dynamic_slice_in_dim(prev_embed, (1 - p) * half, half, 0)
        arrived = [mine, other]
        for a in range(1, cols):
            near = shift(mine, cols - a)
            arrived += [near, trade(near)]
        beside = swap(next_embed, 1)
        across = [swap(next_embed[first : first + step], 2) for first in starts]
        corner = [swap(x, 1) for x in across]
        nexts = [
            [(next_embed, first), (x, 0), (beside, first), (y, 0)]
            for first, x, y in zip(starts, across, corner)
        ]
        places = [((r ^ o) - c + cols) % cols for o in (0, 2, 1, 3)] + [p, 1 - p]
        arrived = jnp.stack(arrived).reshape(cols, 2, half, share)
        prev, prev_t = arrange(arrived, jnp.stack(places).astype(jnp.int32))
        pieces = (
            (0, share, jnp.float32),
            (share, share, jnp.float32),
            (2 * share, 2 * share, jnp.bfloat16),
        )
    else:
        prev = lax.all_gather(prev_embed, "col", axis=1, tiled=True)
        prev_t = prev.T
        gathered = lax.all_gather(next_embed, "row", axis=1, tiled=True)
        nexts = [[(gathered, first)] for first in starts]
        pieces = ((0, features, jnp.float32),)

    bias = log_norm[:, None] * LOG2E
    total = jnp.zeros((rows, 128), jnp.float32)
    for first, nxt in zip(starts, nexts):
        total = row_dots(grad_table, prev, nxt, bias, total, first, step, coef)
    dots = jnp.sum(total, axis=1)
    if paired:
        mine = dots.reshape(rows // 128, 128)
        dots = (mine + sum(shift(mine, a) for a in range(1, cols))).reshape(rows)
    else:
        dots = lax.psum(dots, "col")
    dots = dots[:, None]

    def block(sums, col):
        code = jnp.bitwise_xor(col, r)
        place = jnp.where(code == 1, 2, jnp.where(code == 2, 1, code))
        return lax.dynamic_slice_in_dim(sums, place * share, share, 1)

    def shares(sums):
        return [block(sums, (c + a) % cols).astype(jnp.bfloat16) for a in range(1, cols)]

    def collect(sums, away):
        kept = block(sums, c)
        for a in range(1, cols):
            kept = kept + shift(away[a - 1], a).astype(jnp.float32)
        return kept

    bias = bias - math.log2(scale)
    total = jnp.zeros((rows, features), jnp.float32)
    ends, sent = [], []
    for k, (first, nxt) in enumerate(zip(starts, nexts)):
        if paired and k >= 2:
            total, sent[k - 2] = lax.optimization_barrier((total, sent[k - 2]))
        if paired and k >= 3:
            total, ends[k - 3] = lax.optimization_barrier((total, ends[k - 3]))
        common = (grad_table, prev, prev_t, nxt, bias, dots)
        if paired and k == len(starts) - 1:
            upper, carry = grad_terms(
                *common, total, first, step, coef, ((0, features, jnp.float32),), (), 2, 0
            )
            total, upper_away = lax.optimization_barrier((total, shares(upper)))
            upper_grad = collect(upper, upper_away)
            total, *sums = grad_terms(*common, total, first, step, coef, pieces, (carry,), 2, 1)
        else:
            total, *sums = grad_terms(*common, total, first, step, coef, pieces)
        if paired:
            own, far, give = sums
            got = swap(give, 1)
            sent.append((far + got[:, share:].astype(jnp.float32)).astype(jnp.bfloat16))
            ends.append(own + got[:, :share].astype(jnp.float32))
            if k >= 1:
                ends[k - 1] = ends[k - 1] + swap(sent[k - 1], 2).astype(jnp.float32)
        else:
            ends.append(lax.psum_scatter(sums[0], "row", scatter_dimension=1, tiled=True))
    if paired:
        sent[-1], away = lax.optimization_barrier((sent[-1], shares(total)))
        ends[-1] = ends[-1] + swap(sent[-1], 2).astype(jnp.float32)
        prev_grad = jnp.concatenate([upper_grad, collect(total, away)], axis=0)
    else:
        prev_grad = lax.psum_scatter(total, "col", scatter_dimension=1, tiled=True)
    next_grad = jnp.concatenate(ends, axis=0)
    return (prev_grad, next_grad)


def solution(mesh):
    placed = (P(("parts", "row"), "col"), P("row", "col"), P("col", "row"), P(("parts", "row")))
    return jax.shard_map(
        functools.partial(body, *(mesh.shape[axis] for axis in ("parts", "col", "row"))),
        mesh=mesh,
        in_specs=placed,
        out_specs=(P(("parts", "row"), "col"), P(("parts", "col"), "row")),
        check_vma=False,
    )
```

```python
import functools
import math

import jax
import jax.numpy as jnp
from jax import lax
from jax.experimental import pallas as pl
from jax.experimental.pallas import tpu as pltpu
from jax.sharding import PartitionSpec as P

LOG2E = math.log2(math.e)
TILE = 512
ROW_BLOCK = 256
CHUNKS = 4
NT = (((1,), (1,)), ((), ()))


def arrange_kernel(places_ref, arrived_ref, prev_ref, prev_t_ref):
    block = arrived_ref[0, 0]
    prev_ref[...] = block
    prev_t_ref[...] = block.T


def arrange(arrived, places):
    blocks, halves, height, share = arrived.shape
    rows, features = halves * height, blocks * share
    return pl.pallas_call(
        arrange_kernel,
        grid_spec=pltpu.PrefetchScalarGridSpec(
            num_scalar_prefetch=1,
            grid=(blocks, halves),
            in_specs=[
                pl.BlockSpec(
                    (1, 1, height, share),
                    lambda i, h, places: (places[i], places[blocks + h], 0, 0),
                )
            ],
            out_specs=[
                pl.BlockSpec((height, share), lambda i, h, places: (h, i)),
                pl.BlockSpec((share, height), lambda i, h, places: (i, h)),
            ],
        ),
        out_shape=[
            jax.ShapeDtypeStruct((rows, features), arrived.dtype),
            jax.ShapeDtypeStruct((features, rows), arrived.dtype),
        ],
        cost_estimate=pl.CostEstimate(
            flops=0, bytes_accessed=6 * rows * features, transcendentals=0
        ),
    )(places, arrived)


def join(next_refs, held):
    left = 0
    for ref in next_refs:
        held[:, left : left + ref.shape[1]] = ref[...]
        left += ref.shape[1]


def dots_kernel(coef, count, grad_ref, prev_ref, bias_ref, total_ref, *rest):
    next_refs, (out_ref, next_held) = rest[:count], rest[count:]

    @pl.when(pl.program_id(0) == 0)
    def _():
        out_ref[...] = total_ref[...]

    join(next_refs, next_held)
    rows, width = grad_ref.shape
    block = min(ROW_BLOCK, rows)
    for top in range(0, rows, block):
        here = pl.ds(top, block)
        logits = lax.dot_general(
            prev_ref[here, :], next_held[...], NT, preferred_element_type=jnp.float32
        )
        terms = grad_ref[here, :].astype(jnp.float32) * jnp.exp2(logits * coef - bias_ref[here, :])
        part = terms[:, :128]
        for left in range(128, width, 128):
            part = part + terms[:, left : left + 128]
        out_ref[here, :] += part


def grads_kernel(
    coef, pieces, count, carried, grad_ref, prev_ref, prev_t_ref, bias_ref, dot_ref, total_ref, *rest
):
    next_refs = rest[:count]
    out_ref, *piece_refs = rest[count + carried : -2]
    next_held, held = rest[-2:]

    @pl.when(pl.program_id(0) == 0)
    def _():
        out_ref[...] = total_ref[...]

    join(next_refs, next_held)
    rows = grad_ref.shape[0]
    block = min(ROW_BLOCK, rows)
    for top in range(0, rows, block):
        here = pl.ds(top, block)
        logits = lax.dot_general(
            prev_ref[here, :], next_held[...], NT, preferred_element_type=jnp.float32
        )
        scaled = jnp.exp2(logits * coef - bias_ref[here, :])
        shifted = grad_ref[here, :].astype(jnp.float32) - dot_ref[here, :]
        dlogits = (scaled * shifted).astype(jnp.bfloat16)
        held[here, :] = dlogits
        out_ref[here, :] += jnp.dot(dlogits, next_held[...], preferred_element_type=jnp.float32)
    flipped = jnp.dot(prev_t_ref[...], held[...], preferred_element_type=jnp.float32)
    for (start, size, kind), ref in zip(pieces, piece_refs):
        value = flipped[start : start + size, :].T
        if carried:
            value = value + rest[count][:, start : start + size]
        ref[...] = value.astype(kind)


def whole(shape):
    return pl.BlockSpec(shape, lambda j: (0, 0))


def tiles_of(tile, nexts):
    return [
        pl.BlockSpec((tile, x.shape[1]), functools.partial(lambda skip, j: (j + skip, 0), at // tile))
        for x, at in nexts
    ]


def row_dots(grad, prev, nexts, bias, total, first, step, coef):
    rows, features = prev.shape
    tile = min(TILE, step)
    offset = first // tile
    return pl.pallas_call(
        functools.partial(dots_kernel, coef, len(nexts)),
        grid=(step // tile,),
        out_shape=jax.ShapeDtypeStruct(total.shape, jnp.float32),
        in_specs=[
            pl.BlockSpec((rows, tile), lambda j: (0, j + offset)),
            whole(prev.shape),
            whole(bias.shape),
            whole(total.shape),
        ]
        + tiles_of(tile, nexts),
        out_specs=whole(total.shape),
        scratch_shapes=[pltpu.VMEM((tile, features), jnp.bfloat16)],
        compiler_params=pltpu.CompilerParams(vmem_limit_bytes=48 << 20),
        cost_estimate=pl.CostEstimate(
            flops=2 * rows * step * features,
            bytes_accessed=2 * rows * step,
            transcendentals=rows * step,
        ),
    )(grad, prev, bias, total, *[x for x, _ in nexts])


def grad_terms(
    grad, prev, prev_t, nexts, bias, dots, total, first, step, coef, pieces,
    carry=(), split=1, part=0,
):
    features = prev.shape[1]
    rows = prev.shape[0] // split
    tile = min(TILE, step)
    offset = first // tile
    tall = lambda width: pl.BlockSpec((rows, width), lambda j: (part, 0))
    shape = (rows, features)
    return pl.pallas_call(
        functools.partial(grads_kernel, coef, pieces, len(nexts), len(carry)),
        grid=(step // tile,),
        out_shape=[jax.ShapeDtypeStruct(shape, jnp.float32)]
        + [jax.ShapeDtypeStruct((step, size), kind) for _, size, kind in pieces],
        in_specs=[
            pl.BlockSpec((rows, tile), lambda j: (part, j + offset)),
            tall(features),
            pl.BlockSpec((features, rows), lambda j: (0, part)),
            tall(1),
            tall(1),
            tall(features),
        ]
        + tiles_of(tile, nexts)
        + [pl.BlockSpec((tile, features), lambda j: (j, 0)) for _ in carry],
        out_specs=[whole(shape)]
        + [pl.BlockSpec((tile, size), lambda j: (j, 0)) for _, size, _ in pieces],
        scratch_shapes=[
            pltpu.VMEM((tile, features), jnp.bfloat16),
            pltpu.VMEM((rows, tile), jnp.bfloat16),
        ],
        compiler_params=pltpu.CompilerParams(vmem_limit_bytes=56 << 20),
        cost_estimate=pl.CostEstimate(
            flops=6 * rows * step * features,
            bytes_accessed=2 * rows * step,
            transcendentals=rows * step,
        ),
    )(grad, prev, prev_t, bias, dots, total, *[x for x, _ in nexts], *carry)


def body(parts, cols, grid_rows, grad_table, prev_embed, next_embed, log_norm):
    rows, columns = grad_table.shape
    features = prev_embed.shape[1] * cols
    scale = 2.0 / math.sqrt(features)
    coef = scale * LOG2E
    share = next_embed.shape[1]
    paired = parts == 2 and cols == 4 and grid_rows == 4 and share % 128 == 0
    step = columns // CHUNKS if columns % (CHUNKS * TILE) == 0 else columns
    starts = list(range(0, columns, step))
    r, c, p = lax.axis_index("row"), lax.axis_index("col"), lax.axis_index("parts")

    def swap(x, bit):
        return lax.ppermute(x, "row", [(i, i ^ bit) for i in range(grid_rows)])

    def shift(x, by):
        return lax.ppermute(x, "col", [(i, (i + by) % cols) for i in range(cols)])

    def trade(x):
        return lax.ppermute(x, "parts", [(0, 1), (1, 0)])

    if paired:
        half = rows // 2
        mine = lax.dynamic_slice_in_dim(prev_embed, p * half, half, 0)
        other = lax.dynamic_slice_in_dim(prev_embed, (1 - p) * half, half, 0)
        arrived = [mine, other]
        for a in range(1, cols):
            near = shift(mine, cols - a)
            arrived += [near, trade(near)]
        beside = swap(next_embed, 1)
        across = [swap(next_embed[first : first + step], 2) for first in starts]
        corner = [swap(x, 1) for x in across]
        nexts = [
            [(next_embed, first), (x, 0), (beside, first), (y, 0)]
            for first, x, y in zip(starts, across, corner)
        ]
        places = [((r ^ o) - c + cols) % cols for o in (0, 2, 1, 3)] + [p, 1 - p]
        arrived = jnp.stack(arrived).reshape(cols, 2, half, share)
        prev, prev_t = arrange(arrived, jnp.stack(places).astype(jnp.int32))
        pieces = (
            (0, share, jnp.float32),
            (share, share, jnp.float32),
            (2 * share, 2 * share, jnp.bfloat16),
        )
    else:
        prev = lax.all_gather(prev_embed, "col", axis=1, tiled=True)
        prev_t = prev.T
        gathered = lax.all_gather(next_embed, "row", axis=1, tiled=True)
        nexts = [[(gathered, first)] for first in starts]
        pieces = ((0, features, jnp.float32),)

    bias = log_norm[:, None] * LOG2E
    total = jnp.zeros((rows, 128), jnp.float32)
    for first, nxt in zip(starts, nexts):
        total = row_dots(grad_table, prev, nxt, bias, total, first, step, coef)
    dots = jnp.sum(total, axis=1)
    if paired:
        mine = dots.reshape(rows // 128, 128)
        dots = (mine + sum(shift(mine, a) for a in range(1, cols))).reshape(rows)
    else:
        dots = lax.psum(dots, "col")
    dots = dots[:, None]

    def block(sums, col):
        code = jnp.bitwise_xor(col, r)
        place = jnp.where(code == 1, 2, jnp.where(code == 2, 1, code))
        return lax.dynamic_slice_in_dim(sums, place * share, share, 1)

    def shares(sums):
        return [block(sums, (c + a) % cols).astype(jnp.bfloat16) for a in range(1, cols)]

    def collect(sums, away):
        kept = block(sums, c)
        for a in range(1, cols):
            kept = kept + shift(away[a - 1], a).astype(jnp.float32)
        return kept

    bias = bias - math.log2(scale)
    total = jnp.zeros((rows, features), jnp.float32)
    ends, sent = [], []
    for k, (first, nxt) in enumerate(zip(starts, nexts)):
        if paired and k >= 2:
            total, sent[k - 2] = lax.optimization_barrier((total, sent[k - 2]))
        if paired and k >= 3:
            total, ends[k - 3] = lax.optimization_barrier((total, ends[k - 3]))
        common = (grad_table, prev, prev_t, nxt, bias, dots)
        if paired and k == len(starts) - 1:
            upper, carry = grad_terms(
                *common, total, first, step, coef, ((0, features, jnp.float32),), (), 2, 0
            )
            total, upper_away = lax.optimization_barrier((total, shares(upper)))
            upper_grad = collect(upper, upper_away)
            total, *sums = grad_terms(*common, total, first, step, coef, pieces, (carry,), 2, 1)
        else:
            total, *sums = grad_terms(*common, total, first, step, coef, pieces)
        if paired:
            own, far, give = sums
            got = swap(give, 1)
            sent.append((far + got[:, share:].astype(jnp.float32)).astype(jnp.bfloat16))
            ends.append(own + got[:, :share].astype(jnp.float32))
            if k >= 1:
                ends[k - 1] = ends[k - 1] + swap(sent[k - 1], 2).astype(jnp.float32)
        else:
            ends.append(lax.psum_scatter(sums[0], "row", scatter_dimension=1, tiled=True))
    if paired:
        sent[-1], away = lax.optimization_barrier((sent[-1], shares(total)))
        ends[-1] = ends[-1] + swap(sent[-1], 2).astype(jnp.float32)
        prev_grad = jnp.concatenate([upper_grad, collect(total, away)], axis=0)
    else:
        prev_grad = lax.psum_scatter(total, "col", scatter_dimension=1, tiled=True)
    next_grad = jnp.concatenate(ends, axis=0)
    return (prev_grad, next_grad)


def solution(mesh):
    placed = (P(("parts", "row"), "col"), P("row", "col"), P("col", "row"), P(("parts", "row")))
    return jax.shard_map(
        functools.partial(body, *(mesh.shape[axis] for axis in ("parts", "col", "row"))),
        mesh=mesh,
        in_specs=placed,
        out_specs=(P(("parts", "row"), "col"), P(("parts", "col"), "row")),
        check_vma=False,
    )
```
